256 devices in a mesh: patch: 32 (over y, z_lo, x), head: 8 (over z_hi, core).
Axes of the slice: x: 4, y: 4, z: 8 (z_hi: 4, z_lo: 2; z = z_hi * 2 + z_lo), core: 2. Of those that a mesh axis runs over, the one named last changes fastest.
Arguments:
- fresh_qkv: bfloat16 [16384, 9216], P(('patch', 'head')), may hold values from -500 to 500
- stale_kv: bfloat16 [16384, 2, 3072], P('patch', None, 'head'), may hold values from -100 to 100
- qk_gain: float32 [2, 128], replicated, may hold values from 1 to 2
- patch_len: int32 [32], replicated, may hold values from 384 to 512, as said below
- gate_table: float32 [50, 3072], replicated, may hold values from 4 to 16
- timestep: int32 [1], replicated, may hold values from 0 to 49
Outputs:
- gated: bfloat16 [16384, 3072], P(('patch', 'head'))
The draws below stay inside these ranges and needn't reach their ends.
Inputs may be any that keep to these rules, and one draw needn't show every extreme that they name: Positions of patch p at or past patch_len[p] are padding; some patch is full.
All inputs are finite; a program needn't handle non-finite values.
Results may differ from the reference program's by a relative error of at most 0.01.
Values may be sent and summed in bfloat16 or wider, within the bound.
A program may use at most 128 MiB of HBM per device.

```python
import math
import jax
import jax.numpy as jnp
from jax import lax

HEADS = 24
HD = 128
STEPS = 50
D = 3072
TOK_P = 512
TOKENS = 16384
N_PATCH = 32


def draw_fresh_qkv(key, part):
    key = jax.random.fold_in(key, 11)
    first_key, second_key, third_key = jax.random.split(key, 3)
    draws = jnp.clip(jax.random.normal(first_key, (TOKENS, 3, HEADS, HD), jnp.float32), -5.0, 5.0)
    row_scale = jnp.exp(jax.random.uniform(second_key, (TOKENS, 2, HEADS, 1), jnp.float32, 0.0, math.log(10.0)))
    col_scale = jnp.exp(jax.random.uniform(third_key, (1, 2, HEADS, HD), jnp.float32, 0.0, math.log(10.0)))
    scaled = jnp.concatenate([draws[:, :2] * row_scale * col_scale, draws[:, 2:]], axis=1)
    return scaled.reshape(TOKENS, 3 * HEADS * HD).astype(jnp.bfloat16)


def draw_stale_kv(key, part):
    key = jax.random.fold_in(key, 23)
    draws = jnp.clip(1.3 * jax.random.normal(key, (TOKENS, 2, HEADS, HD), jnp.float32), -6.5, 6.5)
    return draws.reshape(TOKENS, 2, HEADS * HD).astype(jnp.bfloat16)


def draw_patch_len(key, part):
    key = jax.random.fold_in(key, 37)
    first_key, second_key = jax.random.split(key)
    lengths = jax.random.randint(first_key, (N_PATCH,), TOK_P * 3 // 4, TOK_P + 1)
    full_patch = jax.random.randint(second_key, (), 0, N_PATCH)
    return jnp.where(jnp.arange(N_PATCH) == full_patch, TOK_P, lengths).astype(jnp.int32)


def setup_inputs(seed: int = 0) -> dict:
    streams_of = jax.random.split(jax.random.key(seed), 7)
    fresh_qkv = draw_fresh_qkv(jax.random.fold_in(streams_of[6], 71), 0)
    stale_kv = draw_stale_kv(jax.random.fold_in(streams_of[6], 71), 0)
    qk_gain = jnp.clip(jax.random.uniform(streams_of[2], (2, HD), jnp.float32, 1.0, 2.0), 1.0, 2.0)
    patch_len = draw_patch_len(jax.random.fold_in(streams_of[6], 71), 0)
    gate_table = jnp.clip(jnp.exp(jax.random.uniform(streams_of[4], (STEPS, D), jnp.float32, math.log(4.0), math.log(16.0))), 4.0, 16.0)
    timestep = jax.random.randint(streams_of[5], (1,), 0, STEPS).astype(jnp.int32)
    return dict(fresh_qkv=fresh_qkv, stale_kv=stale_kv, qk_gain=qk_gain, patch_len=patch_len, gate_table=gate_table, timestep=timestep)


eps = 1e-06
neg_floor = -1e+30

def normalize(values, gain):
    widened = values.astype(jnp.float32)
    inverse = lax.rsqrt(lax.optimization_barrier(jnp.mean(widened * widened, axis=-1, keepdims=True)) + eps)
    return (widened * inverse * gain).astype(jnp.bfloat16)

def attend(head_queries, head_keys, head_values, key_live):
    scores = jnp.einsum('qd,kd->qk', head_queries.astype(jnp.float32), head_keys.astype(jnp.float32)) * HD ** (-0.5)
    scores = jnp.where(key_live[None, :], scores, neg_floor)
    highest = lax.optimization_barrier(jnp.max(scores, axis=1, keepdims=True))
    weights = jnp.where(key_live[None, :], jnp.exp(scores - highest), 0.0)
    denominator = lax.optimization_barrier(jnp.sum(weights, axis=1, keepdims=True))
    numerator = jnp.dot(weights.astype(jnp.bfloat16), head_values, preferred_element_type=jnp.float32)
    return (numerator / denominator).astype(jnp.bfloat16)

def reference(fresh_qkv, stale_kv, qk_gain, patch_len, gate_table, timestep):
    projected = fresh_qkv.reshape(TOKENS, 3, HEADS, HD)
    queries = normalize(projected[:, 0], qk_gain[0])
    fresh_keys = normalize(projected[:, 1], qk_gain[1])
    fresh_values = projected[:, 2]
    stale = stale_kv.reshape(TOKENS, 2, HEADS, HD)
    positions = jnp.arange(TOK_P, dtype=jnp.int32)
    key_live = (positions[None, :] < patch_len[:, None]).reshape(TOKENS)

    def per_patch(patch_index):
        first_row = (patch_index * TOK_P).astype(jnp.int32)
        own_queries = lax.dynamic_slice_in_dim(queries, first_row, TOK_P, 0)
        all_keys = lax.dynamic_update_slice_in_dim(stale[:, 0], lax.dynamic_slice_in_dim(fresh_keys, first_row, TOK_P, 0), first_row, 0)
        all_values = lax.dynamic_update_slice_in_dim(stale[:, 1], lax.dynamic_slice_in_dim(fresh_values, first_row, TOK_P, 0), first_row, 0)

        def per_head(head_items):
            return attend(head_items[0], head_items[1], head_items[2], key_live)
        outcome = lax.map(per_head, (own_queries.transpose(1, 0, 2), all_keys.transpose(1, 0, 2), all_values.transpose(1, 0, 2)))
        return outcome.transpose(1, 0, 2).reshape(TOK_P, HEADS * HD)
    blocks = lax.map(per_patch, jnp.arange(N_PATCH, dtype=jnp.int32))
    attended = blocks.reshape(TOKENS, HEADS * HD)
    gate_row = lax.dynamic_slice_in_dim(gate_table, timestep[0], 1, 0)
    return (attended.astype(jnp.float32) * gate_row).astype(jnp.bfloat16)
```

```python
import functools
import math

import jax
import jax.numpy as jnp
from jax import lax
from jax.experimental import pallas as pl
from jax.experimental.pallas import tpu as pltpu
from jax.sharding import PartitionSpec as P

F32 = jnp.float32
BF16 = jnp.bfloat16
MESH = pl.DeviceIdType.MESH
EPS = 1e-06
DEAD = -1e30
HD = 128
TOK = 512
ROWS = 64
GROUPS = 8
NH = 3
WIDTH = 3072
SLOTS = 8
QS = 4
MSG = TOK + 32
TQ = 256
LIVE = 384
SCALE = math.log2(math.e) / math.sqrt(HD)
NT = (((1,), (1,)), ((), ()))


def kernel(
    fresh, stale, gain, lens, gate, out,
    qsend, ksend, qbuf, kbuf, vbuf, osend, orecv, att, ret, bias,
    s0, s1, p0, p1, m0, m1, otile, ltile,
    qa_s, qa_r, fa_s, fa_r, z_s, z_r, w_s, w_r, f_s, f_r, qg_s, qg_r, og_s, og_r, oa_s, oa_r, loc,
):
    patch = lax.axis_index("patch")
    g = lax.axis_index("head")
    core = lax.rem(g, 2)
    y, zl, x = patch // 8, lax.rem(patch // 4, 2), lax.rem(patch, 4)
    a = x + core * (y - x)
    b = y + core * (x - y)

    def place(a_, zl_, b_):
        return a_ * (1 + 7 * core) + b_ * (8 - 7 * core) + zl_ * 4

    def along_a(d):
        return (place(lax.rem(a + d, 4), zl, b), g)

    def along_b(d):
        return (place(a, zl, lax.rem(b + d, 4)), g)

    def group(d):
        return lax.rem(g + d, GROUPS)

    other_zl = (place(a, 1 - zl, b), g)

    lane = lax.broadcasted_iota(jnp.int32, (1, HD), 1) + LIVE
    for slot in range(SLOTS + 1):
        d, dz = (0, 0) if slot == SLOTS else (slot % 4, slot // 4)
        source = place(lax.rem(a + 4 - d, 4), lax.rem(zl + dz, 2), b)
        bias[slot : slot + 1, :] = jnp.where(lane < lens[source], 0.0, DEAD)

    def fill(i, _):
        rows = pl.ds(pl.multiple_of(i * TOK, TOK), TOK)
        for h in range(NH):
            vbuf[h, rows, HD:] = jnp.ones((TOK, HD), BF16)
        return 0

    lax.fori_loop(0, SLOTS + 1, fill, 0)

    barrier = pltpu.get_barrier_semaphore()
    peers = [(patch, group(d)) for d in range(1, GROUPS)]
    peers += [along_a(d) for d in range(1, 4)] + [along_b(d) for d in range(1, 4)] + [other_zl]
    for peer in peers:
        pl.semaphore_signal(barrier, inc=1, device_id=peer, device_id_type=MESH)
    pl.semaphore_wait(barrier, len(peers))

    def remote(src, dst, ss, rs, dev):
        return pltpu.make_async_remote_copy(
            src_ref=src, dst_ref=dst, send_sem=ss, recv_sem=rs, device_id=dev, device_id_type=MESH
        )

    def slot_rows(slot):
        return pl.ds(slot * TOK, TOK)

    def kv_slot(t, h, slot):
        return kbuf.at[h, slot_rows(slot)] if t == 0 else vbuf.at[h, slot_rows(slot), pl.ds(0, HD)]

    def zl_copy(t, h):
        return remote(stale.at[h, t], kv_slot(t, h, 4), z_s.at[h, t], z_r.at[h, t], other_zl)

    def own_copy(t, h, d):
        return remote(stale.at[h, t], kv_slot(t, h, d), w_s.at[h, t, d], w_r.at[h, t, d], along_a(d))

    def forward_copy(t, h, d):
        return remote(
            kv_slot(t, h, 4), kv_slot(t, h, 4 + d), f_s.at[h, t, d], f_r.at[h, t, d], along_a(d)
        )

    def columns(base, gg, h):
        return pl.ds(pl.multiple_of(base + (gg * NH + h) * HD, HD), HD)

    def token_rows(gg):
        return pl.ds(pl.multiple_of(gg * ROWS, ROWS), ROWS)

    def q_copy(h, d, src_g=None):
        to = group(d)
        return remote(
            qsend.at[:, columns(0, to, h)],
            qbuf.at[h, 0, token_rows(g if src_g is None else src_g)],
            qa_s.at[h, d], qa_r.at[h, d], (patch, to),
        )

    def fresh_copy(t, h, d, src_g=None):
        to = group(d)
        rows = token_rows(g if src_g is None else src_g)
        if t == 0:
            return remote(
                ksend.at[:, columns(0, to, h)], kbuf.at[h, rows],
                fa_s.at[h, t, d], fa_r.at[h, t, d], (patch, to),
            )
        return remote(
            fresh.at[:, columns(2 * WIDTH, to, h)], vbuf.at[h, rows, pl.ds(0, HD)],
            fa_s.at[h, t, d], fa_r.at[h, t, d], (patch, to),
        )

    def query_copy(h, d):
        return remote(qbuf.at[h, 0], qbuf.at[h, d], qg_s.at[h, d], qg_r.at[h, d], along_b(d))

    def partial_copy(h, d):
        return remote(
            osend.at[h, d - 1], orecv.at[h, d - 1], og_s.at[h, d], og_r.at[h, d], along_b(4 - d)
        )

    def out_copy(h, d, src_g=None):
        to = group(d)
        return remote(
            att.at[h, token_rows(to)],
            ret.at[:, columns(0, g if src_g is None else src_g, h)],
            oa_s.at[h, d], oa_r.at[h, d], (patch, to),
        )

    def arrived(copy_of, *args):
        d = args[-1]
        copy_of(*args, src_g=lax.rem(g + GROUPS - d, GROUPS)).wait_recv()

    def own_local(t, h):
        return pltpu.make_async_copy(stale.at[h, t], kv_slot(t, h, SLOTS), loc.at[h, t])

    def start_stale(h):
        for t in range(2):
            zl_copy(t, h).start()
        for d in (1, 3, 2):
            for t in range(2):
                own_copy(t, h, d).start()

    def start_forward(h):
        for t in range(2):
            zl_copy(t, h).wait_recv()
        for d in (1, 3, 2):
            for t in range(2):
                forward_copy(t, h, d).start()

    start_stale(0)

    def norm(base, which, dst):
        def one(i, _):
            cols = pl.ds(pl.multiple_of(base + i * HD, HD), HD)
            wide = fresh[:, cols].astype(F32)
            inverse = lax.rsqrt(jnp.mean(wide * wide, axis=-1, keepdims=True) + EPS)
            scaled = wide * inverse * gain[which : which + 1, :]
            dst[:, pl.ds(pl.multiple_of(i * HD, HD), HD)] = scaled.astype(BF16)
            return 0

        lax.fori_loop(0, GROUPS * NH, one, 0)

    norm(0, 0, qsend)
    for h in range(NH):
        for d in range(1, GROUPS):
            q_copy(h, d).start()
        qbuf[h, 0, token_rows(g), :] = qsend[:, columns(0, g, h)]
    start_stale(1)
    norm(WIDTH, 1, ksend)
    for h in range(NH):
        kbuf[h, token_rows(g), :] = ksend[:, columns(0, g, h)]
        vbuf[h, token_rows(g), 0:HD] = fresh[:, columns(2 * WIDTH, g, h)]
        for t in range(2):
            own_local(t, h).start()

    def start_queries(h):
        for d in range(1, GROUPS):
            arrived(q_copy, h, d)
        for d in range(1, 4):
            query_copy(h, d).start()

    start_queries(0)
    start_forward(0)
    start_stale(2)
    for h in range(1, NH):
        start_queries(h)
    for h in range(NH):
        for t in range(2):
            for d in range(1, GROUPS):
                fresh_copy(t, h, d).start()
    for h in range(NH):
        for t in range(2):
            own_local(t, h).wait()

    def await_keys(h):
        for t in range(2):
            for d in range(1, 4):
                own_copy(t, h, d).wait_recv()
                forward_copy(t, h, d).wait_recv()

    def await_fresh(h):
        for t in range(2):
            for d in range(1, GROUPS):
                arrived(fresh_copy, t, h, d)

    n_far = NH * (QS - 1)
    n_units = NH * QS

    def unit(u):
        own = u >= n_far
        h = jnp.where(own, u - n_far, u // (QS - 1))
        j = jnp.where(own, 0, lax.rem(u, QS - 1) + 1)
        return h, j, jnp.where(own, 0, 1)

    def score(h, j, first, r, s_ref, m_ref):
        q = qbuf[h, j, r : r + TQ, :]
        top = None
        for s in range(SLOTS):
            rows = pl.ds(pl.multiple_of((first + s) * TOK, TOK), TOK)
            sc = lax.dot_general(q, kbuf[h, rows, :], NT, preferred_element_type=F32)
            parts = [sc[:, i * HD : (i + 1) * HD] for i in range(TOK // HD)]
            parts[-1] = parts[-1] + bias[pl.ds(first + s, 1), :]
            for i, part in enumerate(parts):
                s_ref[:, s * TOK + i * HD : s * TOK + (i + 1) * HD] = part
                top = part if top is None else jnp.maximum(top, part)
        m_ref[...] = jnp.broadcast_to(jnp.max(top, axis=1, keepdims=True) * SCALE, (TQ, HD))

    def weigh(h, first, r, s_ref, m_ref, p_ref):
        high = m_ref[...]
        for i in range(SLOTS * TOK // HD):
            cols = slice(i * HD, (i + 1) * HD)
            p_ref[:, cols] = jnp.exp2(s_ref[:, cols] * SCALE - high).astype(BF16)
        rows = pl.ds(pl.multiple_of(first * TOK, TOK), SLOTS * TOK)
        both = jnp.dot(p_ref[...], vbuf[h, rows, :], preferred_element_type=F32)
        total = both[:, HD:]
        otile[r : r + TQ, :] = both[:, :HD] / total
        ltile[r : r + TQ, :] = high + jnp.log2(total)

    diagonal = lax.broadcasted_iota(jnp.int32, (HD, HD), 0) == lax.broadcasted_iota(
        jnp.int32, (HD, HD), 1
    )

    def send_partial(h, j):
        osend[h, j - 1, 0:TOK, :] = otile[...].astype(BF16)
        logs = jnp.concatenate(
            [
                jnp.sum(jnp.where(diagonal, ltile[i * HD : (i + 1) * HD, :], 0.0), axis=0, keepdims=True)
                for i in range(TOK // HD)
            ]
            + [jnp.zeros((4, HD), F32)],
            axis=0,
        )
        high = logs.astype(BF16).astype(F32)
        middle = (logs - high).astype(BF16).astype(F32)
        low = logs - high - middle
        packed = jnp.concatenate([high, middle, low, jnp.zeros((8, HD), F32)], axis=0)
        osend[h, j - 1, TOK:MSG, :] = packed.astype(BF16)
        partial_copy(h, j).start()

    def merge(h):
        logs = []
        for d in range(1, QS):
            partial_copy(h, d).wait_recv()
            packed = orecv[h, d - 1, TOK:MSG, :].astype(F32)
            logs.append(packed[0:8] + packed[8:16] + packed[16:24])
        for i in range(TOK // HD):
            rows = slice(i * HD, (i + 1) * HD)
            spread = [ltile[rows, :]] + [
                jnp.transpose(jnp.broadcast_to(log[i : i + 1, :], (HD, HD))) for log in logs
            ]
            top = functools.reduce(jnp.maximum, spread)
            shares = [jnp.exp2(one - top) for one in spread]
            total = functools.reduce(jnp.add, shares)
            mixed = shares[0] * otile[rows, :]
            for d in range(1, QS):
                mixed = mixed + shares[d] * orecv[h, d - 1, rows, :].astype(F32)
            att[h, rows, :] = (mixed / total).astype(BF16)
        for d in range(1, GROUPS):
            out_copy(h, d).start()
        ret[:, columns(0, g, h)] = att[h, token_rows(g), :]

    await_keys(0)
    query_copy(0, 1).wait_recv()
    score(0, 1, 1, 0, s0, m0)

    def step(u, _):
        h, j, first = unit(u)
        later = jnp.minimum(u + 1, n_units - 1)
        h2, j2, first2 = unit(later)

        @pl.when(u == 0)
        def _():
            start_forward(1)

        @pl.when(u == 2)
        def _():
            start_forward(2)

        score(h, j, first, TQ, s1, m1)
        weigh(h, first, 0, s0, m0, p0)

        @pl.when(u + 1 < n_far)
        def _():
            query_copy(h2, j2).wait_recv()

        @pl.when((u + 1 < n_far) & (j2 == 1))
        def _():
            await_keys(h2)

        @pl.when((u + 1 >= n_far) & (u + 1 < n_units))
        def _():
            await_fresh(h2)

        score(h2, j2, first2, 0, s0, m0)
        weigh(h, first, TQ, s1, m1, p1)

        @pl.when(u < n_far)
        def _():
            send_partial(h, j)

        @pl.when(u >= n_far)
        def _():
            merge(h)

        return 0

    lax.fori_loop(0, n_units, step, 0)

    for h in range(NH):
        for d in range(1, GROUPS):
            arrived(out_copy, h, d)
    out[...] = (ret[...].astype(F32) * gate[...]).astype(BF16)

    for h in range(NH):
        for d in range(1, GROUPS):
            q_copy(h, d).wait_send()
            out_copy(h, d).wait_send()
            for t in range(2):
                fresh_copy(t, h, d).wait_send()
        for t in range(2):
            zl_copy(t, h).wait_send()
            for d in range(1, 4):
                own_copy(t, h, d).wait_send()
                forward_copy(t, h, d).wait_send()
        for d in range(1, 4):
            query_copy(h, d).wait_send()
            partial_copy(h, d).wait_send()


def local(fresh_qkv, stale_kv, qk_gain, patch_len, gate_table, timestep):
    stale = stale_kv.reshape(TOK, 2, NH, HD).transpose(2, 1, 0, 3)
    gate = lax.dynamic_slice_in_dim(gate_table, timestep[0], 1, 0)
    dma = pltpu.SemaphoreType.DMA
    vmem = pl.BlockSpec(memory_space=pltpu.VMEM)
    keys = (SLOTS + 1) * TOK
    return pl.pallas_call(
        kernel,
        out_shape=jax.ShapeDtypeStruct((ROWS, WIDTH), BF16),
        in_specs=[vmem, vmem, vmem, pl.BlockSpec(memory_space=pltpu.SMEM), vmem],
        out_specs=vmem,
        scratch_shapes=[
            pltpu.VMEM((ROWS, WIDTH), BF16),
            pltpu.VMEM((ROWS, WIDTH), BF16),
            pltpu.VMEM((NH, QS, TOK, HD), BF16),
            pltpu.VMEM((NH, keys, HD), BF16),
            pltpu.VMEM((NH, keys, 2 * HD), BF16),
            pltpu.VMEM((NH, QS - 1, MSG, HD), BF16),
            pltpu.VMEM((NH, QS - 1, MSG, HD), BF16),
            pltpu.VMEM((NH, TOK, HD), BF16),
            pltpu.VMEM((ROWS, WIDTH), BF16),
            pltpu.VMEM((16, HD), F32),
            pltpu.VMEM((TQ, SLOTS * TOK), F32),
            pltpu.VMEM((TQ, SLOTS * TOK), F32),
            pltpu.VMEM((TQ, SLOTS * TOK), BF16),
            pltpu.VMEM((TQ, SLOTS * TOK), BF16),
            pltpu.VMEM((TQ, HD), F32),
            pltpu.VMEM((TQ, HD), F32),
            pltpu.VMEM((TOK, HD), F32),
            pltpu.VMEM((TOK, HD), F32),
            dma((NH, GROUPS)), dma((NH, GROUPS)),
            dma((NH, 2, GROUPS)), dma((NH, 2, GROUPS)),
            dma((NH, 2)), dma((NH, 2)),
            dma((NH, 2, 4)), dma((NH, 2, 4)),
            dma((NH, 2, 4)), dma((NH, 2, 4)),
            dma((NH, 4)), dma((NH, 4)),
            dma((NH, 4)), dma((NH, 4)),
            dma((NH, GROUPS)), dma((NH, GROUPS)),
            dma((NH, 2)),
        ],
        compiler_params=pltpu.CompilerParams(
            collective_id=0, has_side_effects=True, vmem_limit_bytes=56 << 20
        ),
    )(fresh_qkv, stale, qk_gain, patch_len, gate)


def solution(mesh):
    return jax.shard_map(
        local,
        mesh=mesh,
        in_specs=(P(("patch", "head"), None), P("patch", None, "head"), P(), P(), P(), P()),
        out_specs=P(("patch", "head"), None),
        check_vma=False,
    )
```

```python
import functools
import math

import jax
import jax.numpy as jnp
from jax import lax
from jax.experimental import pallas as pl
from jax.experimental.pallas import tpu as pltpu
from jax.sharding import PartitionSpec as P

F32 = jnp.float32
BF16 = jnp.bfloat16
MESH = pl.DeviceIdType.MESH
EPS = 1e-06
DEAD = -1e30
HD = 128
TOK = 512
ROWS = 64
GROUPS = 8
NH = 3
WIDTH = 3072
SLOTS = 9
QS = 4
MSG = TOK + 32
CHUNK = 4
OWN = 4
FAR = 5
LIVE = 384
SCALE = math.log2(math.e) / math.sqrt(HD)
NT = (((1,), (1,)), ((), ()))


def kernel(
    fresh, stale, gain, lens, out,
    qsend, ksend, qbuf, kbuf, vbuf, osend, orecv, att, ret, bias,
    s0, s1, p0, p1, m0, m1, otile, ltile, ohalf, lhalf,
    qa_s, qa_r, fa_s, fa_r, z_s, z_r, w_s, w_r, f_s, f_r, qg_s, qg_r, og_s, og_r, oa_s, oa_r,
):
    patch = lax.axis_index("patch")
    g = lax.axis_index("head")
    core = lax.rem(g, 2)
    y, zl, x = patch // 8, lax.rem(patch // 4, 2), lax.rem(patch, 4)
    a = x + core * (y - x)
    b = y + core * (x - y)

    def place(a_, zl_, b_):
        return a_ * (1 + 7 * core) + b_ * (8 - 7 * core) + zl_ * 4

    def along_a(d):
        return (place(lax.rem(a + d, 4), zl, b), g)

    def along_b(d):
        return (place(a, zl, lax.rem(b + d, 4)), g)

    def group(d):
        return lax.rem(g + d, GROUPS)

    other_zl = (place(a, 1 - zl, b), g)

    barrier = pltpu.get_barrier_semaphore()
    peers = [(patch, group(d)) for d in range(1, GROUPS)]
    peers += [along_a(d) for d in range(1, 4)] + [along_b(d) for d in range(1, 4)] + [other_zl]
    for peer in peers:
        pl.semaphore_signal(barrier, inc=1, device_id=peer, device_id_type=MESH)

    def slot_rows(slot):
        return pl.ds(slot * TOK, TOK)

    def split(h):
        cols = slice(h * HD, (h + 1) * HD)
        kbuf[h, slot_rows(OWN), :] = stale[:, 0, cols]
        vbuf[h, slot_rows(OWN), 0:HD] = stale[:, 1, cols]

    def norm(base, which, dst):
        def one(i, _):
            cols = pl.ds(pl.multiple_of(base + i * HD, HD), HD)
            wide = fresh[:, cols].astype(F32)
            inverse = lax.rsqrt(jnp.mean(wide * wide, axis=-1, keepdims=True) + EPS)
            scaled = wide * inverse * gain[which : which + 1, :]
            dst[:, pl.ds(pl.multiple_of(i * HD, HD), HD)] = scaled.astype(BF16)
            return 0

        lax.fori_loop(0, GROUPS * NH, one, 0)

    split(0)
    norm(0, 0, qsend)
    lane = lax.broadcasted_iota(jnp.int32, (1, HD), 1) + LIVE
    for slot in range(SLOTS):
        d, dz = (slot % OWN, 0) if slot < FAR else (slot - FAR, 1)
        source = place(lax.rem(a + 4 - d, 4), lax.rem(zl + dz, 2), b)
        bias[slot : slot + 1, :] = jnp.where(lane < lens[source], 0.0, DEAD)

    def fill(i, _):
        rows = pl.ds(pl.multiple_of(i * TOK, TOK), TOK)
        for h in range(NH):
            vbuf[h, rows, HD:] = jnp.ones((TOK, HD), BF16)
        return 0

    lax.fori_loop(0, SLOTS, fill, 0)
    pl.semaphore_wait(barrier, len(peers))

    def remote(src, dst, ss, rs, dev):
        return pltpu.make_async_remote_copy(
            src_ref=src, dst_ref=dst, send_sem=ss, recv_sem=rs, device_id=dev, device_id_type=MESH
        )

    def kv_slot(t, h, slot):
        return kbuf.at[h, slot_rows(slot)] if t == 0 else vbuf.at[h, slot_rows(slot), pl.ds(0, HD)]

    def zl_copy(t, h):
        return remote(kv_slot(t, h, OWN), kv_slot(t, h, FAR), z_s, z_r.at[h, t], other_zl)

    def side_copy(t, h, d, far):
        ss, rs = (f_s, f_r) if far else (w_s, w_r)
        src, dst = (FAR, FAR + d) if far else (OWN, d)
        return remote(kv_slot(t, h, src), kv_slot(t, h, dst), ss, rs.at[h, t, d], along_a(d))

    def relay_copy(t, h):
        d = (1, 3)[t]
        return remote(kv_slot(t, h, d), kv_slot(t, h, 2), w_s, w_r.at[h, t, 2], along_a(d))

    def columns(base, gg, h):
        return pl.ds(pl.multiple_of(base + (gg * NH + h) * HD, HD), HD)

    def token_rows(gg):
        return pl.ds(pl.multiple_of(gg * ROWS, ROWS), ROWS)

    def q_copy(h, d):
        to = group(d)
        return remote(
            qsend.at[:, columns(0, to, h)], qbuf.at[h, 0, token_rows(g)], qa_s, qa_r.at[h], (patch, to)
        )

    def fresh_copy(t, h, d):
        to = group(d)
        rows = token_rows(g)
        if t == 0:
            src, dst = ksend.at[:, columns(0, to, h)], kbuf.at[h, rows]
        else:
            src, dst = fresh.at[:, columns(2 * WIDTH, to, h)], vbuf.at[h, rows, pl.ds(0, HD)]
        return remote(src, dst, fa_s.at[t], fa_r.at[h, t], (patch, to))

    def query_copy(h, d):
        return remote(qbuf.at[h, 0], qbuf.at[h, d], qg_s, qg_r.at[h, d], along_b(d))

    def partial_copy(h, d):
        return remote(osend.at[h, d - 1], orecv.at[h, d - 1], og_s, og_r.at[h, d], along_b(4 - d))

    def out_copy(h, d):
        to = group(d)
        return remote(
            att.at[h, token_rows(to)], ret.at[:, columns(0, g, h)], oa_s, oa_r.at[h], (patch, to)
        )

    def wait_all(ref, sem):
        pltpu.make_async_copy(ref, ref, sem).wait()

    others = (GROUPS - 1) * ROWS

    def start_zl(h):
        for t in range(2):
            zl_copy(t, h).start()

    def start_side(h, far):
        for t in range(2):
            for d in (1, 3, 2) if far else (1, 3):
                side_copy(t, h, d, far).start()

    def start_relay(h):
        side_copy(0, h, 1, 0).wait_recv()
        relay_copy(0, h).start()
        side_copy(1, h, 3, 0).wait_recv()
        relay_copy(1, h).start()

    def start_forward(h):
        for t in range(2):
            zl_copy(t, h).wait_recv()
        start_side(h, 1)

    def start_q(h):
        for d in range(1, GROUPS):
            q_copy(h, d).start()

    def start_queries(h):
        wait_all(qbuf.at[h, 0, pl.ds(0, others)], qa_r.at[h])
        for d in (1, 3, 2):
            query_copy(h, d).start()

    def start_fresh(h):
        for t in range(2):
            for d in range(1, GROUPS):
                fresh_copy(t, h, d).start()

    for h in range(NH):
        start_q(h)
        if h < 2:
            start_side(h, 0)
        if h == 0:
            split(1)
            split(2)
    for h in range(NH):
        start_zl(h)
    norm(WIDTH, 1, ksend)
    for h in range(NH):
        start_fresh(h)
    for h in range(NH):
        qbuf[h, 0, token_rows(g), :] = qsend[:, columns(0, g, h)]
        kbuf[h, token_rows(g), :] = ksend[:, columns(0, g, h)]
        vbuf[h, token_rows(g), 0:HD] = fresh[:, columns(2 * WIDTH, g, h)]
    start_relay(0)
    start_queries(0)
    start_side(2, 0)
    start_relay(1)

    events = {
        0: [(start_queries, 1)],
        1: [(start_relay, 2)],
        2: [(start_queries, 2)],
        3: [(start_forward, 0)],
        6: [(start_forward, 1)],
        9: [(start_forward, 2)],
    }

    def await_keys(h, far):
        side_copy(0, h, 3, far).wait_recv()
        side_copy(1, h, 1, far).wait_recv()
        if far:
            side_copy(0, h, 1, far).wait_recv()
            side_copy(1, h, 3, far).wait_recv()
        for t in range(2):
            side_copy(t, h, 2, far).wait_recv()

    def await_fresh(h):
        wait_all(kbuf.at[h, pl.ds(0, others)], fa_r.at[h, 0])
        wait_all(vbuf.at[h, pl.ds(0, others), pl.ds(0, HD)], fa_r.at[h, 1])

    n_half = NH * (QS - 1)
    n_own = 2 * n_half
    n_steps = 2 * NH * QS

    def unit(t):
        own = t >= n_own
        far = jnp.where(own, lax.rem(t - n_own, 2), t // n_half)
        r = lax.rem(t, n_half)
        h = jnp.where(own, (t - n_own) // 2, r // (QS - 1))
        j = jnp.where(own, 0, lax.rem(r, QS - 1) + 1)
        first = jnp.where(far == 1, FAR, jnp.where(own, 0, 1))
        return h, j, first, far

    def score(h, j, first, s_ref, m_ref):
        q = qbuf[h, j]
        top = None
        for s in range(CHUNK):
            rows = pl.ds(pl.multiple_of((first + s) * TOK, TOK), TOK)
            sc = lax.dot_general(q, kbuf[h, rows, :], NT, preferred_element_type=F32)
            parts = [sc[:, i * HD : (i + 1) * HD] for i in range(TOK // HD)]
            parts[-1] = parts[-1] + bias[pl.ds(first + s, 1), :]
            for i, part in enumerate(parts):
                s_ref[:, s * TOK + i * HD : s * TOK + (i + 1) * HD] = part
                top = part if top is None else jnp.maximum(top, part)
        m_ref[...] = jnp.broadcast_to(jnp.max(top, axis=1, keepdims=True) * SCALE, (TOK, HD))

    def weigh(h, first, s_ref, m_ref, p_ref):
        high = m_ref[...]
        for i in range(CHUNK * TOK // HD):
            cols = slice(i * HD, (i + 1) * HD)
            p_ref[:, cols] = jnp.exp2(s_ref[:, cols] * SCALE - high).astype(BF16)
        rows = pl.ds(pl.multiple_of(first * TOK, TOK), CHUNK * TOK)
        both = jnp.dot(p_ref[...], vbuf[h, rows, :], preferred_element_type=F32)
        total = both[:, HD:]
        otile[...] = both[:, :HD] / total
        ltile[...] = high + jnp.log2(total)

    def join(h, j):
        near, here = lhalf[h, j], ltile[...]
        top = jnp.maximum(near, here)
        w_near, w_here = jnp.exp2(near - top), jnp.exp2(here - top)
        total = w_near + w_here
        otile[...] = (w_near * ohalf[h, j] + w_here * otile[...]) / total
        ltile[...] = top + jnp.log2(total)

    diagonal = lax.broadcasted_iota(jnp.int32, (HD, HD), 0) == lax.broadcasted_iota(
        jnp.int32, (HD, HD), 1
    )

    def send_partial(h, j):
        osend[h, j - 1, 0:TOK, :] = otile[...].astype(BF16)
        logs = jnp.concatenate(
            [
                jnp.sum(jnp.where(diagonal, ltile[i * HD : (i + 1) * HD, :], 0.0), axis=0, keepdims=True)
                for i in range(TOK // HD)
            ]
            + [jnp.zeros((4, HD), F32)],
            axis=0,
        )
        high = logs.astype(BF16).astype(F32)
        middle = (logs - high).astype(BF16).astype(F32)
        low = logs - high - middle
        packed = jnp.concatenate([high, middle, low, jnp.zeros((8, HD), F32)], axis=0)
        osend[h, j - 1, TOK:MSG, :] = packed.astype(BF16)
        partial_copy(h, j).start()

    def merge(h):
        logs = []
        for d in range(1, QS):
            partial_copy(h, d).wait_recv()
            packed = orecv[h, d - 1, TOK:MSG, :].astype(F32)
            logs.append(packed[0:8] + packed[8:16] + packed[16:24])
        for i in range(TOK // HD):
            rows = slice(i * HD, (i + 1) * HD)
            spread = [ltile[rows, :]] + [
                jnp.transpose(jnp.broadcast_to(log[i : i + 1, :], (HD, HD))) for log in logs
            ]
            top = functools.reduce(jnp.maximum, spread)
            shares = [jnp.exp2(one - top) for one in spread]
            total = functools.reduce(jnp.add, shares)
            mixed = shares[0] * otile[rows, :]
            for d in range(1, QS):
                mixed = mixed + shares[d] * orecv[h, d - 1, rows, :].astype(F32)
            att[h, rows, :] = (mixed / total).astype(BF16)
        for d in range(1, GROUPS):
            out_copy(h, d).start()
        ret[:, columns(0, g, h)] = att[h, token_rows(g), :]

    def await_inputs(t, h, j, far):
        @pl.when((t < n_half) & (j == 1))
        def _():
            await_keys(h, 0)

        @pl.when(t < n_half)
        def _():
            query_copy(h, j).wait_recv()

        @pl.when((t >= n_half) & (t < n_own) & (j == 1))
        def _():
            await_keys(h, 1)

        @pl.when((t >= n_own) & (far == 0))
        def _():
            await_fresh(h)

    def finish(h, j, far):
        @pl.when(far == 0)
        def _():
            ohalf[h, j] = otile[...]
            lhalf[h, j] = ltile[...]

        @pl.when((far == 1) & (j > 0))
        def _():
            join(h, j)
            send_partial(h, j)

        @pl.when((far == 1) & (j == 0))
        def _():
            join(h, j)
            merge(h)

    await_keys(0, 0)
    query_copy(0, 1).wait_recv()
    score(0, 1, 1, s0, m0)

    def pair(u, _):
        for half, (s_in, m_in, p, s_out, m_out) in enumerate(((s0, m0, p0, s1, m1), (s1, m1, p1, s0, m0))):
            t = 2 * u + half
            for when, calls in events.items():
                if when % 2 == half:

                    @pl.when(u == when // 2)
                    def _(calls=calls):
                        for call, *args in calls:
                            call(*args)

            h, j, first, far = unit(t)
            later = t + 1
            if half == 1:
                later = jnp.minimum(later, n_steps - 1)
            h2, j2, first2, far2 = unit(later)
            if half == 1:

                @pl.when(t + 1 < n_steps)
                def _():
                    await_inputs(later, h2, j2, far2)

            else:
                await_inputs(later, h2, j2, far2)
            score(h2, j2, first2, s_out, m_out)
            weigh(h, first, s_in, m_in, p)
            finish(h, j, far)
        return 0

    lax.fori_loop(0, n_steps // 2, pair, 0)

    for h in range(NH):
        wait_all(att.at[h, pl.ds(0, others)], oa_r.at[h])
    out[...] = ret[...]

    wait_all(kbuf.at[0, pl.ds(0, NH * others)], qa_s)
    for t in range(2):
        wait_all(kbuf.at[0, pl.ds(0, NH * others)], fa_s.at[t])
    wait_all(kbuf.at[0, pl.ds(0, NH * others)], oa_s)
    wait_all(kbuf.at[0, pl.ds(0, NH * 2 * TOK)], z_s)
    wait_all(kbuf.at[pl.ds(0, 2)], w_s)
    wait_all(kbuf.at[pl.ds(0, 2)], f_s)
    wait_all(kbuf.at[0], qg_s)
    wait_all(orecv, og_s)


def local(fresh_qkv, stale_kv, qk_gain, patch_len, gate_table, timestep):
    dma = pltpu.SemaphoreType.DMA
    vmem = pl.BlockSpec(memory_space=pltpu.VMEM)
    keys = SLOTS * TOK
    returned = pl.pallas_call(
        kernel,
        out_shape=jax.ShapeDtypeStruct((ROWS, WIDTH), BF16),
        in_specs=[vmem, vmem, vmem, pl.BlockSpec(memory_space=pltpu.SMEM)],
        out_specs=vmem,
        scratch_shapes=[
            pltpu.VMEM((ROWS, WIDTH), BF16),
            pltpu.VMEM((ROWS, WIDTH), BF16),
            pltpu.VMEM((NH, QS, TOK, HD), BF16),
            pltpu.VMEM((NH, keys, HD), BF16),
            pltpu.VMEM((NH, keys, 2 * HD), BF16),
            pltpu.VMEM((NH, QS - 1, MSG, HD), BF16),
            pltpu.VMEM((NH, QS - 1, MSG, HD), BF16),
            pltpu.VMEM((NH, TOK, HD), BF16),
            pltpu.VMEM((ROWS, WIDTH), BF16),
            pltpu.VMEM((16, HD), F32),
            pltpu.VMEM((TOK, CHUNK * TOK), F32),
            pltpu.VMEM((TOK, CHUNK * TOK), F32),
            pltpu.VMEM((TOK, CHUNK * TOK), BF16),
            pltpu.VMEM((TOK, CHUNK * TOK), BF16),
            pltpu.VMEM((TOK, HD), F32),
            pltpu.VMEM((TOK, HD), F32),
            pltpu.VMEM((TOK, HD), F32),
            pltpu.VMEM((TOK, HD), F32),
            pltpu.VMEM((NH, QS, TOK, HD), F32),
            pltpu.VMEM((NH, QS, TOK, HD), F32),
            dma, dma((NH,)),
            dma((2,)), dma((NH, 2)),
            dma, dma((NH, 2)),
            dma, dma((NH, 2, 4)),
            dma, dma((NH, 2, 4)),
            dma, dma((NH, 4)),
            dma, dma((NH, 4)),
            dma, dma((NH,)),
        ],
        compiler_params=pltpu.CompilerParams(
            collective_id=0, has_side_effects=True, vmem_limit_bytes=56 << 20
        ),
    )(fresh_qkv, stale_kv, qk_gain, patch_len)
    gate_row = lax.dynamic_slice_in_dim(gate_table, timestep[0], 1, 0)
    return (returned.astype(F32) * gate_row).astype(BF16)


def solution(mesh):
    return jax.shard_map(
        local,
        mesh=mesh,
        in_specs=(P(("patch", "head"), None), P("patch", None, "head"), P(), P(), P(), P()),
        out_specs=P(("patch", "head"), None),
        check_vma=False,
    )
```

```python
import functools
import math

import jax
import jax.numpy as jnp
from jax import lax
from jax.experimental import pallas as pl
from jax.experimental.pallas import tpu as pltpu
from jax.sharding import PartitionSpec as P

F32 = jnp.float32
BF16 = jnp.bfloat16
MESH = pl.DeviceIdType.MESH
EPS = 1e-06
DEAD = -1e30
HD = 128
TOK = 512
ROWS = 64
GROUPS = 8
NH = 3
WIDTH = 3072
SLOTS = 9
QS = 4
MSG = TOK + 32
CHUNK = 4
OWN = 4
FAR = 5
LIVE = 384
SCALE = math.log2(math.e) / math.sqrt(HD)
NT = (((1,), (1,)), ((), ()))


def kernel(
    fresh, stale, gain, lens, out,
    qsend, ksend, qbuf, kbuf, vbuf, osend, orecv, att, ret, bias,
    s0, s1, p0, p1, m0, m1, otile, ltile, ohalf, lhalf, kstage, vstage,
    qa_s, qa_r, fa_s, fa_r, z_s, z_r, w_s, w_r, f_s, f_r, qg_s, qg_r, og_s, og_r, oa_s, oa_r,
):
    patch = lax.axis_index("patch")
    g = lax.axis_index("head")
    core = lax.rem(g, 2)
    y, zl, x = patch // 8, lax.rem(patch // 4, 2), lax.rem(patch, 4)
    a = x + core * (y - x)
    b = y + core * (x - y)

    def place(a_, zl_, b_):
        return a_ * (1 + 7 * core) + b_ * (8 - 7 * core) + zl_ * 4

    def along_a(d):
        return (place(lax.rem(a + d, 4), zl, b), g)

    def along_b(d):
        return (place(a, zl, lax.rem(b + d, 4)), g)

    def group(d):
        return lax.rem(g + d, GROUPS)

    other_zl = (place(a, 1 - zl, b), g)

    barrier = pltpu.get_barrier_semaphore()
    peers = [(patch, group(d)) for d in range(1, GROUPS)]
    peers += [along_a(d) for d in range(1, 4)] + [along_b(d) for d in range(1, 4)] + [other_zl]
    for peer in peers:
        pl.semaphore_signal(barrier, inc=1, device_id=peer, device_id_type=MESH)

    def slot_rows(slot):
        return pl.ds(slot * TOK, TOK)

    def split(h):
        cols = slice(h * HD, (h + 1) * HD)
        kbuf[h, slot_rows(OWN), :] = stale[:, 0, cols]
        vbuf[h, slot_rows(OWN), 0:HD] = stale[:, 1, cols]

    def norm(base, which, dst):
        def one(i, _):
            cols = pl.ds(pl.multiple_of(base + i * HD, HD), HD)
            wide = fresh[:, cols].astype(F32)
            inverse = lax.rsqrt(jnp.mean(wide * wide, axis=-1, keepdims=True) + EPS)
            scaled = wide * inverse * gain[which : which + 1, :]
            dst[:, pl.ds(pl.multiple_of(i * HD, HD), HD)] = scaled.astype(BF16)
            return 0

        lax.fori_loop(0, GROUPS * NH, one, 0)

    split(0)
    norm(0, 0, qsend)
    lane = lax.broadcasted_iota(jnp.int32, (1, HD), 1) + LIVE
    for slot in range(SLOTS):
        d, dz = (slot % OWN, 0) if slot < FAR else (slot - FAR, 1)
        source = place(lax.rem(a + 4 - d, 4), lax.rem(zl + dz, 2), b)
        bias[slot : slot + 1, :] = jnp.where(lane < lens[source], 0.0, DEAD)

    def fill(i, _):
        rows = pl.ds(pl.multiple_of(i * TOK, TOK), TOK)
        for h in range(NH):
            vbuf[h, rows, HD:] = jnp.ones((TOK, HD), BF16)
        return 0

    lax.fori_loop(0, SLOTS, fill, 0)
    pl.semaphore_wait(barrier, len(peers))

    def remote(src, dst, ss, rs, dev):
        return pltpu.make_async_remote_copy(
            src_ref=src, dst_ref=dst, send_sem=ss, recv_sem=rs, device_id=dev, device_id_type=MESH
        )

    def kv_slot(t, h, slot):
        return kbuf.at[h, slot_rows(slot)] if t == 0 else vbuf.at[h, slot_rows(slot), pl.ds(0, HD)]

    def zl_copy(t, h):
        return remote(kv_slot(t, h, OWN), kv_slot(t, h, FAR), z_s, z_r.at[h, t], other_zl)

    def side_copy(t, h, d, far):
        ss, rs = (f_s, f_r) if far else (w_s, w_r)
        src, dst = (FAR, FAR + d) if far else (OWN, d)
        return remote(kv_slot(t, h, src), kv_slot(t, h, dst), ss, rs.at[h, t, d], along_a(d))

    def relay_copy(t, h):
        d = (1, 3)[t]
        return remote(kv_slot(t, h, d), kv_slot(t, h, 2), w_s, w_r.at[h, t, 2], along_a(d))

    def columns(base, gg, h):
        return pl.ds(pl.multiple_of(base + (gg * NH + h) * HD, HD), HD)

    def token_rows(gg):
        return pl.ds(pl.multiple_of(gg * ROWS, ROWS), ROWS)

    def q_copy(h, d):
        to = group(d)
        return remote(
            qsend.at[:, columns(0, to, h)], qbuf.at[h, 0, token_rows(g)], qa_s, qa_r.at[h], (patch, to)
        )

    def fresh_copy(t, d):
        to = group(d)
        base, src, dst = ((0, ksend, kstage), (2 * WIDTH, fresh, vstage))[t]
        cols = pl.ds(pl.multiple_of(base + to * (NH * HD), HD), NH * HD)
        return remote(src.at[:, cols], dst.at[token_rows(g)], fa_s.at[t], fa_r.at[t], (patch, to))

    def query_copy(h, d):
        return remote(qbuf.at[h, 0], qbuf.at[h, d], qg_s, qg_r.at[h, d], along_b(d))

    def partial_copy(h, d):
        return remote(osend.at[h, d - 1], orecv.at[h, d - 1], og_s, og_r.at[h, d], along_b(4 - d))

    def out_copy(h, d):
        to = group(d)
        return remote(
            att.at[h, token_rows(to)], ret.at[:, columns(0, g, h)], oa_s, oa_r.at[h], (patch, to)
        )

    def wait_all(ref, sem):
        pltpu.make_async_copy(ref, ref, sem).wait()

    others = (GROUPS - 1) * ROWS

    def start_zl(h):
        for t in range(2):
            zl_copy(t, h).start()

    def start_side(h, far):
        for t in range(2):
            for d in (1, 3, 2) if far else (1, 3):
                side_copy(t, h, d, far).start()

    def start_relay(h):
        side_copy(0, h, 1, 0).wait_recv()
        relay_copy(0, h).start()
        side_copy(1, h, 3, 0).wait_recv()
        relay_copy(1, h).start()

    def start_forward(h):
        for t in range(2):
            zl_copy(t, h).wait_recv()
        start_side(h, 1)

    def start_q(h):
        for d in range(1, GROUPS):
            q_copy(h, d).start()

    def start_queries(h):
        wait_all(qbuf.at[h, 0, pl.ds(0, others)], qa_r.at[h])
        for d in (1, 3, 2):
            query_copy(h, d).start()

    def start_fresh():
        for t in range(2):
            for d in range(1, GROUPS):
                fresh_copy(t, d).start()

    start_q(0)
    start_side(0, 0)
    start_q(1)
    qbuf[0, 0, token_rows(g), :] = qsend[:, columns(0, g, 0)]
    split(1)
    start_side(1, 0)
    split(2)
    start_q(2)
    start_relay(0)
    start_queries(0)
    for h in range(NH):
        start_zl(h)
    start_side(2, 0)
    norm(WIDTH, 1, ksend)
    start_fresh()
    for h in range(NH):
        if h > 0:
            qbuf[h, 0, token_rows(g), :] = qsend[:, columns(0, g, h)]
        cols = columns(0, g, h)
        kstage[token_rows(g), h * HD : (h + 1) * HD] = ksend[:, cols]
        vstage[token_rows(g), h * HD : (h + 1) * HD] = fresh[:, columns(2 * WIDTH, g, h)]
    start_relay(1)

    events = {
        0: [(start_queries, 1)],
        1: [(start_relay, 2)],
        2: [(start_queries, 2)],
        3: [(start_forward, 0)],
        6: [(start_forward, 1)],
        9: [(start_forward, 2)],
    }

    def await_keys(h, far):
        side_copy(0, h, 3, far).wait_recv()
        side_copy(1, h, 1, far).wait_recv()
        if far:
            side_copy(0, h, 1, far).wait_recv()
            side_copy(1, h, 3, far).wait_recv()
        for t in range(2):
            side_copy(t, h, 2, far).wait_recv()

    def await_fresh():
        wait_all(kstage.at[pl.ds(0, others)], fa_r.at[0])
        wait_all(vstage.at[pl.ds(0, others)], fa_r.at[1])
        for h in range(NH):
            cols = slice(h * HD, (h + 1) * HD)
            kbuf[h, 0:TOK, :] = kstage[:, cols]
            vbuf[h, 0:TOK, 0:HD] = vstage[:, cols]

    n_half = NH * (QS - 1)
    n_own = 2 * n_half
    n_steps = 2 * NH * QS

    def unit(t):
        own = t >= n_own
        far = jnp.where(own, lax.rem(t - n_own, 2), t // n_half)
        r = lax.rem(t, n_half)
        h = jnp.where(own, (t - n_own) // 2, r // (QS - 1))
        j = jnp.where(own, 0, lax.rem(r, QS - 1) + 1)
        first = jnp.where(far == 1, FAR, jnp.where(own, 0, 1))
        return h, j, first, far

    def score(h, j, first, s_ref, m_ref):
        q = qbuf[h, j]
        top = None
        for s in range(CHUNK):
            rows = pl.ds(pl.multiple_of((first + s) * TOK, TOK), TOK)
            sc = lax.dot_general(q, kbuf[h, rows, :], NT, preferred_element_type=F32)
            parts = [sc[:, i * HD : (i + 1) * HD] for i in range(TOK // HD)]
            parts[-1] = parts[-1] + bias[pl.ds(first + s, 1), :]
            for i, part in enumerate(parts):
                s_ref[:, s * TOK + i * HD : s * TOK + (i + 1) * HD] = part
                top = part if top is None else jnp.maximum(top, part)
        m_ref[...] = jnp.broadcast_to(jnp.max(top, axis=1, keepdims=True) * SCALE, (TOK, HD))

    def weigh(h, first, s_ref, m_ref, p_ref):
        high = m_ref[...]
        for i in range(CHUNK * TOK // HD):
            cols = slice(i * HD, (i + 1) * HD)
            p_ref[:, cols] = jnp.exp2(s_ref[:, cols] * SCALE - high).astype(BF16)
        rows = pl.ds(pl.multiple_of(first * TOK, TOK), CHUNK * TOK)
        both = jnp.dot(p_ref[...], vbuf[h, rows, :], preferred_element_type=F32)
        total = both[:, HD:]
        otile[...] = both[:, :HD] / total
        ltile[...] = high + jnp.log2(total)

    def join(h, j):
        near, here = lhalf[h, j], ltile[...]
        top = jnp.maximum(near, here)
        w_near, w_here = jnp.exp2(near - top), jnp.exp2(here - top)
        total = w_near + w_here
        otile[...] = (w_near * ohalf[h, j] + w_here * otile[...]) / total
        ltile[...] = top + jnp.log2(total)

    diagonal = lax.broadcasted_iota(jnp.int32, (HD, HD), 0) == lax.broadcasted_iota(
        jnp.int32, (HD, HD), 1
    )

    def send_partial(h, j):
        osend[h, j - 1, 0:TOK, :] = otile[...].astype(BF16)
        logs = jnp.concatenate(
            [
                jnp.sum(jnp.where(diagonal, ltile[i * HD : (i + 1) * HD, :], 0.0), axis=0, keepdims=True)
                for i in range(TOK // HD)
            ]
            + [jnp.zeros((4, HD), F32)],
            axis=0,
        )
        high = logs.astype(BF16).astype(F32)
        middle = (logs - high).astype(BF16).astype(F32)
        low = logs - high - middle
        packed = jnp.concatenate([high, middle, low, jnp.zeros((8, HD), F32)], axis=0)
        osend[h, j - 1, TOK:MSG, :] = packed.astype(BF16)
        partial_copy(h, j).start()

    def merge(h):
        logs = []
        for d in range(1, QS):
            partial_copy(h, d).wait_recv()
            packed = orecv[h, d - 1, TOK:MSG, :].astype(F32)
            logs.append(packed[0:8] + packed[8:16] + packed[16:24])
        for i in range(TOK // HD):
            rows = slice(i * HD, (i + 1) * HD)
            spread = [ltile[rows, :]] + [
                jnp.transpose(jnp.broadcast_to(log[i : i + 1, :], (HD, HD))) for log in logs
            ]
            top = functools.reduce(jnp.maximum, spread)
            shares = [jnp.exp2(one - top) for one in spread]
            total = functools.reduce(jnp.add, shares)
            mixed = shares[0] * otile[rows, :]
            for d in range(1, QS):
                mixed = mixed + shares[d] * orecv[h, d - 1, rows, :].astype(F32)
            att[h, rows, :] = (mixed / total).astype(BF16)
        for d in range(1, GROUPS):
            out_copy(h, d).start()
        ret[:, columns(0, g, h)] = att[h, token_rows(g), :]

    def await_inputs(t, h, j, far):
        @pl.when((t < n_half) & (j == 1))
        def _():
            await_keys(h, 0)

        @pl.when(t < n_half)
        def _():
            query_copy(h, j).wait_recv()

        @pl.when((t >= n_half) & (t < n_own) & (j == 1))
        def _():
            await_keys(h, 1)

        @pl.when(t == n_own)
        def _():
            await_fresh()

    def finish(h, j, far):
        @pl.when(far == 0)
        def _():
            ohalf[h, j] = otile[...]
            lhalf[h, j] = ltile[...]

        @pl.when((far == 1) & (j > 0))
        def _():
            join(h, j)
            send_partial(h, j)

        @pl.when((far == 1) & (j == 0))
        def _():
            join(h, j)
            merge(h)

    await_keys(0, 0)
    query_copy(0, 1).wait_recv()
    score(0, 1, 1, s0, m0)

    def pair(u, _):
        for half, (s_in, m_in, p, s_out, m_out) in enumerate(((s0, m0, p0, s1, m1), (s1, m1, p1, s0, m0))):
            t = 2 * u + half
            for when, calls in events.items():
                if when % 2 == half:

                    @pl.when(u == when // 2)
                    def _(calls=calls):
                        for call, *args in calls:
                            call(*args)

            h, j, first, far = unit(t)
            later = t + 1
            if half == 1:
                later = jnp.minimum(later, n_steps - 1)
            h2, j2, first2, far2 = unit(later)
            if half == 1:

                @pl.when(t + 1 < n_steps)
                def _():
                    await_inputs(later, h2, j2, far2)

            else:
                await_inputs(later, h2, j2, far2)
            score(h2, j2, first2, s_out, m_out)
            weigh(h, first, s_in, m_in, p)
            finish(h, j, far)
        return 0

    lax.fori_loop(0, n_steps // 2, pair, 0)

    for h in range(NH):
        wait_all(att.at[h, pl.ds(0, others)], oa_r.at[h])
    out[...] = ret[...]

    wait_all(kbuf.at[0, pl.ds(0, NH * others)], qa_s)
    for t in range(2):
        wait_all(kstage.at[pl.ds(0, others)], fa_s.at[t])
    wait_all(kbuf.at[0, pl.ds(0, NH * others)], oa_s)
    wait_all(kbuf.at[0, pl.ds(0, NH * 2 * TOK)], z_s)
    wait_all(kbuf.at[pl.ds(0, 2)], w_s)
    wait_all(kbuf.at[pl.ds(0, 2)], f_s)
    wait_all(kbuf.at[0], qg_s)
    wait_all(orecv, og_s)


def local(fresh_qkv, stale_kv, qk_gain, patch_len, gate_table, timestep):
    dma = pltpu.SemaphoreType.DMA
    vmem = pl.BlockSpec(memory_space=pltpu.VMEM)
    keys = SLOTS * TOK
    returned = pl.pallas_call(
        kernel,
        out_shape=jax.ShapeDtypeStruct((ROWS, WIDTH), BF16),
        in_specs=[vmem, vmem, vmem, pl.BlockSpec(memory_space=pltpu.SMEM)],
        out_specs=vmem,
        scratch_shapes=[
            pltpu.VMEM((ROWS, WIDTH), BF16),
            pltpu.VMEM((ROWS, WIDTH), BF16),
            pltpu.VMEM((NH, QS, TOK, HD), BF16),
            pltpu.VMEM((NH, keys, HD), BF16),
            pltpu.VMEM((NH, keys, 2 * HD), BF16),
            pltpu.VMEM((NH, QS - 1, MSG, HD), BF16),
            pltpu.VMEM((NH, QS - 1, MSG, HD), BF16),
            pltpu.VMEM((NH, TOK, HD), BF16),
            pltpu.VMEM((ROWS, WIDTH), BF16),
            pltpu.VMEM((16, HD), F32),
            pltpu.VMEM((TOK, CHUNK * TOK), F32),
            pltpu.VMEM((TOK, CHUNK * TOK), F32),
            pltpu.VMEM((TOK, CHUNK * TOK), BF16),
            pltpu.VMEM((TOK, CHUNK * TOK), BF16),
            pltpu.VMEM((TOK, HD), F32),
            pltpu.VMEM((TOK, HD), F32),
            pltpu.VMEM((TOK, HD), F32),
            pltpu.VMEM((TOK, HD), F32),
            pltpu.VMEM((NH, QS, TOK, HD), F32),
            pltpu.VMEM((NH, QS, TOK, HD), F32),
            pltpu.VMEM((TOK, NH * HD), BF16),
            pltpu.VMEM((TOK, NH * HD), BF16),
            dma, dma((NH,)),
            dma((2,)), dma((2,)),
            dma, dma((NH, 2)),
            dma, dma((NH, 2, 4)),
            dma, dma((NH, 2, 4)),
            dma, dma((NH, 4)),
            dma, dma((NH, 4)),
            dma, dma((NH,)),
        ],
        compiler_params=pltpu.CompilerParams(
            collective_id=0, has_side_effects=True, vmem_limit_bytes=56 << 20
        ),
    )(fresh_qkv, stale_kv, qk_gain, patch_len)
    gate_row = lax.dynamic_slice_in_dim(gate_table, timestep[0], 1, 0)
    return (returned.astype(F32) * gate_row).astype(BF16)


def solution(mesh):
    return jax.shard_map(
        local,
        mesh=mesh,
        in_specs=(P(("patch", "head"), None), P("patch", None, "head"), P(), P(), P(), P()),
        out_specs=P(("patch", "head"), None),
        check_vma=False,
    )
```

```python
import functools
import math

import jax
import jax.numpy as jnp
from jax import lax
from jax.experimental import pallas as pl
from jax.experimental.pallas import tpu as pltpu
from jax.sharding import PartitionSpec as P

F32 = jnp.float32
BF16 = jnp.bfloat16
MESH = pl.DeviceIdType.MESH
EPS = 1e-06
DEAD = -1e30
HD = 128
TOK = 512
ROWS = 64
GROUPS = 8
NH = 3
WIDTH = 3072
SLOTS = 9
QS = 4
MSG = TOK + 32
CHUNK = 4
OWN = 4
FAR = 5
LIVE = 384
SCALE = math.log2(math.e) / math.sqrt(HD)
NT = (((1,), (1,)), ((), ()))


def kernel(
    fresh, stale, gain, lens, out,
    qsend, ksend, qbuf, kbuf, vbuf, osend, orecv, att, ret, bias,
    s0, s1, p0, p1, m0, m1, otile, ltile, ohalf, lhalf, kstage, vstage,
    qa_s, qa_r, fa_s, fa_r, z_s, z_r, w_s, w_r, f_s, f_r, qg_s, qg_r, og_s, og_r, oa_s, oa_r,
):
    patch = lax.axis_index("patch")
    g = lax.axis_index("head")
    core = lax.rem(g, 2)
    y, zl, x = patch // 8, lax.rem(patch // 4, 2), lax.rem(patch, 4)
    a = x + core * (y - x)
    b = y + core * (x - y)

    def place(a_, zl_, b_):
        return a_ * (1 + 7 * core) + b_ * (8 - 7 * core) + zl_ * 4

    def along_a(d):
        return (place(lax.rem(a + d, 4), zl, b), g)

    def along_b(d):
        return (place(a, zl, lax.rem(b + d, 4)), g)

    def group(d):
        return lax.rem(g + d, GROUPS)

    other_zl = (place(a, 1 - zl, b), g)

    barrier = pltpu.get_barrier_semaphore()
    peers = [(patch, group(d)) for d in range(1, GROUPS)]
    peers += [along_a(d) for d in range(1, 4)] + [along_b(d) for d in range(1, 4)] + [other_zl]
    for peer in peers:
        pl.semaphore_signal(barrier, inc=1, device_id=peer, device_id_type=MESH)

    def slot_rows(slot):
        return pl.ds(slot * TOK, TOK)

    def split(h):
        cols = slice(h * HD, (h + 1) * HD)
        kbuf[h, slot_rows(OWN), :] = stale[:, 0, cols]
        vbuf[h, slot_rows(OWN), 0:HD] = stale[:, 1, cols]

    def norm(base, which, dst):
        def one(i, _):
            cols = pl.ds(pl.multiple_of(base + i * HD, HD), HD)
            wide = fresh[:, cols].astype(F32)
            inverse = lax.rsqrt(jnp.mean(wide * wide, axis=-1, keepdims=True) + EPS)
            scaled = wide * inverse * gain[which : which + 1, :]
            dst[:, pl.ds(pl.multiple_of(i * HD, HD), HD)] = scaled.astype(BF16)
            return 0

        lax.fori_loop(0, GROUPS * NH, one, 0)

    split(0)
    norm(0, 0, qsend)
    lane = lax.broadcasted_iota(jnp.int32, (1, HD), 1) + LIVE
    for slot in range(SLOTS):
        d, dz = (slot % OWN, 0) if slot < FAR else (slot - FAR, 1)
        source = place(lax.rem(a + 4 - d, 4), lax.rem(zl + dz, 2), b)
        bias[slot : slot + 1, :] = jnp.where(lane < lens[source], 0.0, DEAD)

    def fill(i, _):
        rows = pl.ds(pl.multiple_of(i * TOK, TOK), TOK)
        for h in range(NH):
            vbuf[h, rows, HD:] = jnp.ones((TOK, HD), BF16)
        return 0

    lax.fori_loop(0, SLOTS, fill, 0)
    pl.semaphore_wait(barrier, len(peers))

    def remote(src, dst, ss, rs, dev):
        return pltpu.make_async_remote_copy(
            src_ref=src, dst_ref=dst, send_sem=ss, recv_sem=rs, device_id=dev, device_id_type=MESH
        )

    def kv_slot(t, h, slot):
        return kbuf.at[h, slot_rows(slot)] if t == 0 else vbuf.at[h, slot_rows(slot), pl.ds(0, HD)]

    def zl_copy(t, h):
        return remote(kv_slot(t, h, OWN), kv_slot(t, h, FAR), z_s, z_r.at[h, t], other_zl)

    def side_copy(t, h, d, far):
        ss, rs = (f_s, f_r) if far else (w_s, w_r)
        src, dst = (FAR, FAR + d) if far else (OWN, d)
        return remote(kv_slot(t, h, src), kv_slot(t, h, dst), ss, rs.at[h, t, d], along_a(d))

    def relay_copy(t, h):
        d = (1, 3)[t]
        return remote(kv_slot(t, h, d), kv_slot(t, h, 2), w_s, w_r.at[h, t, 2], along_a(d))

    def columns(base, gg, h):
        return pl.ds(pl.multiple_of(base + (gg * NH + h) * HD, HD), HD)

    def token_rows(gg):
        return pl.ds(pl.multiple_of(gg * ROWS, ROWS), ROWS)

    def q_copy(h, d):
        to = group(d)
        return remote(
            qsend.at[:, columns(0, to, h)], qbuf.at[h, 0, token_rows(g)], qa_s, qa_r.at[h], (patch, to)
        )

    def fresh_copy(t, d):
        to = group(d)
        base, src, dst = ((0, ksend, kstage), (2 * WIDTH, fresh, vstage))[t]
        cols = pl.ds(pl.multiple_of(base + to * (NH * HD), HD), NH * HD)
        return remote(src.at[:, cols], dst.at[token_rows(g)], fa_s.at[t], fa_r.at[t], (patch, to))

    def query_copy(h, d):
        return remote(qbuf.at[h, 0], qbuf.at[h, d], qg_s, qg_r.at[h, d], along_b(d))

    def partial_copy(h, d):
        return remote(osend.at[h, d - 1], orecv.at[h, d - 1], og_s, og_r.at[h, d], along_b(4 - d))

    def out_copy(h, d):
        to = group(d)
        return remote(
            att.at[h, token_rows(to)], ret.at[:, columns(0, g, h)], oa_s, oa_r.at[h], (patch, to)
        )

    def wait_all(ref, sem):
        pltpu.make_async_copy(ref, ref, sem).wait()

    others = (GROUPS - 1) * ROWS

    def start_zl(h):
        for t in range(2):
            zl_copy(t, h).start()

    def start_side(h, far):
        for t in range(2):
            for d in (1, 3, 2) if far else (1, 3):
                side_copy(t, h, d, far).start()

    def start_relay(h):
        side_copy(0, h, 1, 0).wait_recv()
        relay_copy(0, h).start()
        side_copy(1, h, 3, 0).wait_recv()
        relay_copy(1, h).start()

    def start_forward(h):
        for t in range(2):
            zl_copy(t, h).wait_recv()
        start_side(h, 1)

    def start_q(h):
        for d in range(1, GROUPS):
            q_copy(h, d).start()

    def start_queries(h):
        wait_all(qbuf.at[h, 0, pl.ds(0, others)], qa_r.at[h])
        for d in (1, 3, 2):
            query_copy(h, d).start()

    def start_fresh():
        for t in range(2):
            for d in range(1, GROUPS):
                fresh_copy(t, d).start()

    start_q(0)
    start_side(0, 0)
    start_q(1)
    qbuf[0, 0, token_rows(g), :] = qsend[:, columns(0, g, 0)]
    split(1)
    start_side(1, 0)
    split(2)
    start_q(2)
    start_relay(0)
    start_queries(0)
    for h in range(NH):
        start_zl(h)
    start_side(2, 0)
    norm(WIDTH, 1, ksend)
    start_fresh()
    for h in range(NH):
        if h > 0:
            qbuf[h, 0, token_rows(g), :] = qsend[:, columns(0, g, h)]
        cols = columns(0, g, h)
        kstage[token_rows(g), h * HD : (h + 1) * HD] = ksend[:, cols]
        vstage[token_rows(g), h * HD : (h + 1) * HD] = fresh[:, columns(2 * WIDTH, g, h)]
    start_relay(1)

    events = {
        0: [(start_queries, 1)],
        2: [(start_queries, 2)],
        3: [(start_relay, 2), (start_forward, 0)],
        6: [(start_forward, 1)],
        9: [(start_forward, 2)],
    }

    def await_keys(h, far):
        side_copy(0, h, 3, far).wait_recv()
        side_copy(1, h, 1, far).wait_recv()
        if far:
            side_copy(0, h, 1, far).wait_recv()
            side_copy(1, h, 3, far).wait_recv()
        for t in range(2):
            side_copy(t, h, 2, far).wait_recv()

    def await_fresh():
        wait_all(kstage.at[pl.ds(0, others)], fa_r.at[0])
        wait_all(vstage.at[pl.ds(0, others)], fa_r.at[1])
        for h in range(NH):
            cols = slice(h * HD, (h + 1) * HD)
            kbuf[h, 0:TOK, :] = kstage[:, cols]
            vbuf[h, 0:TOK, 0:HD] = vstage[:, cols]

    n_half = NH * (QS - 1)
    n_own = 2 * n_half
    n_steps = 2 * NH * QS

    def unit(t):
        own = t >= n_own
        far = jnp.where(own, lax.rem(t - n_own, 2), t // n_half)
        r = lax.rem(t, n_half)
        h = jnp.where(own, (t - n_own) // 2, r // (QS - 1))
        j = jnp.where(own, 0, lax.rem(r, QS - 1) + 1)
        first = jnp.where(far == 1, FAR, jnp.where(own, 0, 1))
        return h, j, first, far

    def score(h, j, first, s_ref, m_ref):
        q = qbuf[h, j]
        top = None
        for s in range(CHUNK):
            rows = pl.ds(pl.multiple_of((first + s) * TOK, TOK), TOK)
            sc = lax.dot_general(q, kbuf[h, rows, :], NT, preferred_element_type=F32)
            parts = [sc[:, i * HD : (i + 1) * HD] for i in range(TOK // HD)]
            parts[-1] = parts[-1] + bias[pl.ds(first + s, 1), :]
            for i, part in enumerate(parts):
                s_ref[:, s * TOK + i * HD : s * TOK + (i + 1) * HD] = part
                top = part if top is None else jnp.maximum(top, part)
        m_ref[...] = jnp.broadcast_to(jnp.max(top, axis=1, keepdims=True) * SCALE, (TOK, HD))

    def weigh(h, first, s_ref, m_ref, p_ref):
        high = m_ref[...]
        for i in range(CHUNK * TOK // HD):
            cols = slice(i * HD, (i + 1) * HD)
            p_ref[:, cols] = jnp.exp2(s_ref[:, cols] * SCALE - high).astype(BF16)
        rows = pl.ds(pl.multiple_of(first * TOK, TOK), CHUNK * TOK)
        both = jnp.dot(p_ref[...], vbuf[h, rows, :], preferred_element_type=F32)
        total = both[:, HD:]
        otile[...] = both[:, :HD] / total
        ltile[...] = high + jnp.log2(total)

    def join(h, j):
        near, here = lhalf[h, j], ltile[...]
        top = jnp.maximum(near, here)
        w_near, w_here = jnp.exp2(near - top), jnp.exp2(here - top)
        total = w_near + w_here
        otile[...] = (w_near * ohalf[h, j] + w_here * otile[...]) / total
        ltile[...] = top + jnp.log2(total)

    diagonal = lax.broadcasted_iota(jnp.int32, (HD, HD), 0) == lax.broadcasted_iota(
        jnp.int32, (HD, HD), 1
    )

    def send_partial(h, j):
        osend[h, j - 1, 0:TOK, :] = otile[...].astype(BF16)
        logs = jnp.concatenate(
            [
                jnp.sum(jnp.where(diagonal, ltile[i * HD : (i + 1) * HD, :], 0.0), axis=0, keepdims=True)
                for i in range(TOK // HD)
            ]
            + [jnp.zeros((4, HD), F32)],
            axis=0,
        )
        high = logs.astype(BF16).astype(F32)
        middle = (logs - high).astype(BF16).astype(F32)
        low = logs - high - middle
        packed = jnp.concatenate([high, middle, low, jnp.zeros((8, HD), F32)], axis=0)
        osend[h, j - 1, TOK:MSG, :] = packed.astype(BF16)
        partial_copy(h, j).start()

    def merge(h):
        logs = []
        for d in range(1, QS):
            partial_copy(h, d).wait_recv()
            packed = orecv[h, d - 1, TOK:MSG, :].astype(F32)
            logs.append(packed[0:8] + packed[8:16] + packed[16:24])
        for i in range(TOK // HD):
            rows = slice(i * HD, (i + 1) * HD)
            spread = [ltile[rows, :]] + [
                jnp.transpose(jnp.broadcast_to(log[i : i + 1, :], (HD, HD))) for log in logs
            ]
            top = functools.reduce(jnp.maximum, spread)
            shares = [jnp.exp2(one - top) for one in spread]
            total = functools.reduce(jnp.add, shares)
            mixed = shares[0] * otile[rows, :]
            for d in range(1, QS):
                mixed = mixed + shares[d] * orecv[h, d - 1, rows, :].astype(F32)
            att[h, rows, :] = (mixed / total).astype(BF16)
        for d in range(1, GROUPS):
            out_copy(h, d).start()
        ret[:, columns(0, g, h)] = att[h, token_rows(g), :]

    def await_inputs(t, h, j, far):
        @pl.when((t < n_half) & (j == 1))
        def _():
            await_keys(h, 0)

        @pl.when(t < n_half)
        def _():
            query_copy(h, j).wait_recv()

        @pl.when((t >= n_half) & (t < n_own) & (j == 1))
        def _():
            await_keys(h, 1)

        @pl.when(t == n_own)
        def _():
            await_fresh()

    def finish(h, j, far):
        @pl.when(far == 0)
        def _():
            ohalf[h, j] = otile[...]
            lhalf[h, j] = ltile[...]

        @pl.when((far == 1) & (j > 0))
        def _():
            join(h, j)
            send_partial(h, j)

        @pl.when((far == 1) & (j == 0))
        def _():
            join(h, j)
            merge(h)

    await_keys(0, 0)
    query_copy(0, 1).wait_recv()
    score(0, 1, 1, s0, m0)

    def pair(u, _):
        for half, (s_in, m_in, p, s_out, m_out) in enumerate(((s0, m0, p0, s1, m1), (s1, m1, p1, s0, m0))):
            t = 2 * u + half
            for when, calls in events.items():
                if when % 2 == half:

                    @pl.when(u == when // 2)
                    def _(calls=calls):
                        for call, *args in calls:
                            call(*args)

            h, j, first, far = unit(t)
            later = t + 1
            if half == 1:
                later = jnp.minimum(later, n_steps - 1)
            h2, j2, first2, far2 = unit(later)
            if half == 1:

                @pl.when(t + 1 < n_steps)
                def _():
                    await_inputs(later, h2, j2, far2)

            else:
                await_inputs(later, h2, j2, far2)
            score(h2, j2, first2, s_out, m_out)
            weigh(h, first, s_in, m_in, p)
            finish(h, j, far)
        return 0

    lax.fori_loop(0, n_steps // 2, pair, 0)

    for h in range(NH):
        wait_all(att.at[h, pl.ds(0, others)], oa_r.at[h])
    out[...] = ret[...]

    wait_all(kbuf.at[0, pl.ds(0, NH * others)], qa_s)
    for t in range(2):
        wait_all(kstage.at[pl.ds(0, others)], fa_s.at[t])
    wait_all(kbuf.at[0, pl.ds(0, NH * others)], oa_s)
    wait_all(kbuf.at[0, pl.ds(0, NH * 2 * TOK)], z_s)
    wait_all(kbuf.at[pl.ds(0, 2)], w_s)
    wait_all(kbuf.at[pl.ds(0, 2)], f_s)
    wait_all(kbuf.at[0], qg_s)
    wait_all(orecv, og_s)


def local(fresh_qkv, stale_kv, qk_gain, patch_len, gate_table, timestep):
    dma = pltpu.SemaphoreType.DMA
    vmem = pl.BlockSpec(memory_space=pltpu.VMEM)
    keys = SLOTS * TOK
    returned = pl.pallas_call(
        kernel,
        out_shape=jax.ShapeDtypeStruct((ROWS, WIDTH), BF16),
        in_specs=[vmem, vmem, vmem, pl.BlockSpec(memory_space=pltpu.SMEM)],
        out_specs=vmem,
        scratch_shapes=[
            pltpu.VMEM((ROWS, WIDTH), BF16),
            pltpu.VMEM((ROWS, WIDTH), BF16),
            pltpu.VMEM((NH, QS, TOK, HD), BF16),
            pltpu.VMEM((NH, keys, HD), BF16),
            pltpu.VMEM((NH, keys, 2 * HD), BF16),
            pltpu.VMEM((NH, QS - 1, MSG, HD), BF16),
            pltpu.VMEM((NH, QS - 1, MSG, HD), BF16),
            pltpu.VMEM((NH, TOK, HD), BF16),
            pltpu.VMEM((ROWS, WIDTH), BF16),
            pltpu.VMEM((16, HD), F32),
            pltpu.VMEM((TOK, CHUNK * TOK), F32),
            pltpu.VMEM((TOK, CHUNK * TOK), F32),
            pltpu.VMEM((TOK, CHUNK * TOK), BF16),
            pltpu.VMEM((TOK, CHUNK * TOK), BF16),
            pltpu.VMEM((TOK, HD), F32),
            pltpu.VMEM((TOK, HD), F32),
            pltpu.VMEM((TOK, HD), F32),
            pltpu.VMEM((TOK, HD), F32),
            pltpu.VMEM((NH, QS, TOK, HD), F32),
            pltpu.VMEM((NH, QS, TOK, HD), F32),
            pltpu.VMEM((TOK, NH * HD), BF16),
            pltpu.VMEM((TOK, NH * HD), BF16),
            dma, dma((NH,)),
            dma((2,)), dma((2,)),
            dma, dma((NH, 2)),
            dma, dma((NH, 2, 4)),
            dma, dma((NH, 2, 4)),
            dma, dma((NH, 4)),
            dma, dma((NH, 4)),
            dma, dma((NH,)),
        ],
        compiler_params=pltpu.CompilerParams(
            collective_id=0, has_side_effects=True, vmem_limit_bytes=56 << 20
        ),
    )(fresh_qkv, stale_kv, qk_gain, patch_len)
    gate_row = lax.dynamic_slice_in_dim(gate_table, timestep[0], 1, 0)
    return (returned.astype(F32) * gate_row).astype(BF16)


def solution(mesh):
    return jax.shard_map(
        local,
        mesh=mesh,
        in_specs=(P(("patch", "head"), None), P("patch", None, "head"), P(), P(), P(), P()),
        out_specs=P(("patch", "head"), None),
        check_vma=False,
    )
```
